256 devices in a mesh: seq: 64 (over z, x, core), kvh: 4 (over y).
Axes of the slice: x: 4, y: 4, z: 8, core: 2. Of those that a mesh axis runs over, the one named last changes fastest.
Arguments:
- queries: bfloat16 [64, 2, 128, 128], P('seq', None, 'kvh'), may hold values from -64 to 64
- new_keys: bfloat16 [64, 2, 8, 128], P('seq', None, 'kvh'), may hold values from -6 to 6
- new_values: bfloat16 [64, 2, 8, 128], P('seq', None, 'kvh'), may hold values from -6 to 6
- cache_keys: bfloat16 [64, 8192, 8, 128], P('kvh', 'seq'), may hold values from -36 to 36
- cache_values: bfloat16 [64, 8192, 8, 128], P('kvh', 'seq'), may hold values from -6 to 6
- decode_order: int32 [64], replicated, may hold values from 0 to 63, each once
- cache_len: int32 [64], replicated, may hold values from 1 to 8192, as said below
Outputs:
- attended: bfloat16 [64, 2, 128, 128], P('seq', None, 'kvh')
The draws below stay inside these ranges and needn't reach their ends.
Inputs may be any that keep to these rules, and one draw needn't show every extreme that they name: `cache_len`: every row holds at least one valid position, and some row holds all 8192.
All inputs are finite; a program needn't handle non-finite values.
Results may differ from the reference program's by a relative error of at most 0.0045.
Values may be sent and summed in bfloat16 or wider, within the bound.
No kernel may reach another device: no remote copies, remote signals or barrier semaphores. Data moves between devices by JAX's collectives and lax.ppermute only.
A program may use at most 64 MiB of HBM per device.

```python
import jax
import jax.numpy as jnp
from jax import lax

HEADS = 128
KV_HEADS = 8
HEAD_DIM = 128
STEPS = 2
S = 8192
ROWS = 64


def draw_queries(key, part):
    key = jax.random.fold_in(key, 11)
    base = jax.random.normal(key, (ROWS, STEPS, HEADS, HEAD_DIM), jnp.float32)
    return jnp.clip(base, -6.0, 6.0).astype(jnp.bfloat16)


def draw_cache_keys(key, part):
    key = jax.random.fold_in(key, 23)
    base = jax.random.normal(key, (ROWS, S, KV_HEADS, HEAD_DIM), jnp.float32)
    return jnp.clip(base, -6.0, 6.0).astype(jnp.bfloat16)


def draw_cache_len(key, part):
    key = jax.random.fold_in(key, 37)
    lengths = jax.random.randint(key, (ROWS,), 1, S + 1)
    where_full = jax.random.randint(jax.random.fold_in(key, 1), (), 0, ROWS)
    return lengths.at[where_full].set(S).astype(jnp.int32)


def block_levels(key, dims, cuts, low, high):
    loudness = 1.0
    for axis_at, parts in cuts:
        steps = jax.random.uniform(jax.random.fold_in(jax.random.fold_in(key, 6), axis_at), (parts,), jnp.float32, low / len(cuts), high / len(cuts))
        loudness = loudness * jnp.repeat(jnp.exp(steps), dims[axis_at] // parts).reshape((-1,) + (1,) * (len(dims) - 1 - axis_at))
    return loudness


def gaussian(stream_key, extent, deviation, bound, pieces=(), dtype=jnp.bfloat16):
    array = jax.random.normal(stream_key, extent, jnp.float32) * deviation
    if len(pieces) > 0:
        array = block_levels(stream_key, extent, pieces, -0.22, 0.18) * array
    return jnp.clip(array, min=-bound, max=bound).astype(dtype)


def setup_inputs(seed: int = 0) -> dict:
    keys = jax.random.split(jax.random.key(seed), 8)
    queries = draw_queries(jax.random.fold_in(keys[7], 71), 0)
    new_keys = gaussian(keys[1], (ROWS, STEPS, KV_HEADS, HEAD_DIM), 1.0, 6.0, ((0, 64), (2, 4)))
    new_values = gaussian(keys[2], (ROWS, STEPS, KV_HEADS, HEAD_DIM), 1.0, 6.0, ((0, 64), (2, 4)))
    cache_keys = draw_cache_keys(jax.random.fold_in(keys[7], 71), 0)
    cache_values = gaussian(keys[4], (ROWS, S, KV_HEADS, HEAD_DIM), 1.0, 6.0, ((0, 4), (1, 64)))
    decode_order = jax.random.permutation(keys[5], ROWS).astype(jnp.int32)
    cache_len = draw_cache_len(jax.random.fold_in(keys[7], 71), 0)
    return dict(queries=queries, new_keys=new_keys, new_values=new_values, cache_keys=cache_keys, cache_values=cache_values, decode_order=decode_order, cache_len=cache_len)


NEG_FILL = -1.0e30


def reference(queries, new_keys, new_values, cache_keys, cache_values, decode_order, cache_len):
    group = HEADS // KV_HEADS
    scale = HEAD_DIM ** -0.5
    causal = jnp.arange(STEPS)[:, None] >= jnp.arange(STEPS)[None, :]
    causal = causal[:, None, None, :]
    positions = jnp.arange(S)

    def one_row(slot):
        row = decode_order[slot]
        query_f = queries[slot].astype(jnp.float32).reshape(STEPS, KV_HEADS, group, HEAD_DIM)
        keys_f = cache_keys[row].astype(jnp.float32)
        scores = jnp.einsum("tkgd,skd->tkgs", query_f, keys_f) * scale
        valid = positions < cache_len[row]
        scores = jnp.where(valid, scores, NEG_FILL)
        fresh = jnp.einsum("tkgd,ukd->tkgu", query_f, new_keys[slot].astype(jnp.float32)) * scale
        fresh = jnp.where(causal, fresh, NEG_FILL)
        top = jnp.maximum(jnp.max(scores, -1), jnp.max(fresh, -1))
        weights = jnp.where(valid, jnp.exp(scores - top[..., None]), 0.0)
        fresh_weights = jnp.where(causal, jnp.exp(fresh - top[..., None]), 0.0)
        total = jnp.sum(weights, -1) + jnp.sum(fresh_weights, -1)
        rounded = lax.optimization_barrier(weights.astype(jnp.bfloat16))
        fresh_rounded = lax.optimization_barrier(fresh_weights.astype(jnp.bfloat16))
        accum = jnp.einsum("tkgs,skd->tkgd", rounded.astype(jnp.float32), cache_values[row].astype(jnp.float32))
        accum = accum + jnp.einsum("tkgu,ukd->tkgd", fresh_rounded.astype(jnp.float32), new_values[slot].astype(jnp.float32))
        return (accum / total[..., None]).astype(jnp.bfloat16).reshape(STEPS, HEADS, HEAD_DIM)

    return lax.map(one_row, jnp.arange(ROWS))
```

```python
import jax
import jax.numpy as jnp
from jax import lax
from jax.experimental import pallas as pl
from jax.experimental.pallas import tpu as pltpu
from jax.sharding import PartitionSpec as P

NEG_FILL = -1e30
NC, NY = 2, 4
CHIPS = 32
GROUP = 16
ROWS = 8
LINES = 64
TAIL = 8
BLOCK = LINES + TAIL
F32 = jnp.float32
BF16 = jnp.bfloat16
SMEM = pl.BlockSpec(memory_space=pltpu.SMEM)
VMEM = pl.BlockSpec(memory_space=pltpu.VMEM)
PARAMS = pltpu.CompilerParams(vmem_limit_bytes=16 * 2**20)
BRINGING = pl.CostEstimate(flops=2**30, bytes_accessed=2**24, transcendentals=0)


def split_pair(x):
    high = x.astype(BF16).astype(F32)
    low = (x - high).astype(BF16).astype(F32)
    return high, low


def coordinates():
    s = lax.axis_index("seq")
    return s // NC, lax.rem(s, NC), lax.axis_index("kvh")


def spread_kernel(own_ref, out_ref, core_ref):
    for chip in range(CHIPS):
        out_ref[chip] = own_ref[...]
    core_ref[0] = coordinates()[1]


def spread(own):
    return pl.pallas_call(
        spread_kernel,
        in_specs=[VMEM],
        out_specs=[VMEM, SMEM],
        out_shape=[
            jax.ShapeDtypeStruct((CHIPS,) + own.shape, BF16),
            jax.ShapeDtypeStruct((1,), jnp.int32),
        ],
        compiler_params=PARAMS,
    )(own)


def pass_on_kernel(token, got_ref, out_ref, token_out):
    out_ref[...] = got_ref[...]
    token_out[0] = token[0]


def pass_on(token, got):
    return pl.pallas_call(
        pass_on_kernel,
        in_specs=[SMEM, VMEM],
        out_specs=[VMEM, SMEM],
        out_shape=[
            jax.ShapeDtypeStruct(got.shape, got.dtype),
            jax.ShapeDtypeStruct((1,), jnp.int32),
        ],
        compiler_params=PARAMS,
        cost_estimate=BRINGING,
    )(token, got)


def to_groups_kernel(order, own_ref, other_ref, *refs):
    outs, slots = refs[:NY], refs[NY]
    _, core, y = coordinates()
    for slot in range(CHIPS * NC):
        slots[order[slot]] = slot
    for d in range(NY):
        group = lax.rem(y + d, NY)
        for row in range(ROWS):
            slot = slots[(group * NC + core) * ROWS + row]
            chip = slot // NC
            mine = lax.rem(slot, NC) == core
            outs[d][row] = jnp.where(mine, own_ref[chip], other_ref[chip])


def to_groups(order, own, other):
    _, lines, size = own.shape
    return pl.pallas_call(
        to_groups_kernel,
        in_specs=[SMEM, VMEM, VMEM],
        out_specs=[VMEM] * NY,
        out_shape=[jax.ShapeDtypeStruct((ROWS, lines, size), BF16)] * NY,
        scratch_shapes=[pltpu.SMEM((CHIPS * NC,), jnp.int32)],
        compiler_params=PARAMS,
        cost_estimate=BRINGING,
    )(order, own, other)


def by_head_kernel(core, *refs):
    ins, outs = refs[:4], refs[4 : 4 + NY]
    token, keep = refs[-2:]
    _, positions, kv, size = ins[0].shape
    y = coordinates()[2]
    token[0] = core[0]
    for slot in range(4):
        keep[slot] = ins[slot][0].reshape(positions * kv, size).astype(F32)
    for d in range(NY):
        quarter = lax.rem(y + NY - d, NY)
        for k in range(2):
            head = pl.ds(2 * quarter + k, positions, stride=kv)
            for i in range(2):
                outs[d][0, i * 2 + k] = keep[i, head, :].astype(BF16).T
                outs[d][0, 4 + i * 2 + k] = keep[2 + i, head, :].astype(BF16)


def by_head(core, keys, values):
    _, positions, kv, size = keys[0].shape
    rows = pl.BlockSpec((1, positions, kv, size), lambda i, core: (core[0] * ROWS + i, 0, 0, 0))
    tiles = (8, size, positions)
    outs = pl.pallas_call(
        by_head_kernel,
        grid_spec=pltpu.PrefetchScalarGridSpec(
            num_scalar_prefetch=1,
            grid=(ROWS,),
            in_specs=[rows] * 4,
            out_specs=[pl.BlockSpec((1,) + tiles, lambda i, core: (i, 0, 0, 0))] * NY + [SMEM],
            scratch_shapes=[pltpu.VMEM((4, positions * kv, size), F32)],
        ),
        out_shape=[jax.ShapeDtypeStruct((ROWS,) + tiles, BF16)] * NY
        + [jax.ShapeDtypeStruct((1,), jnp.int32)],
        cost_estimate=pl.CostEstimate(
            flops=0, bytes_accessed=16 * ROWS * positions * kv * size, transcendentals=0
        ),
    )(core, *keys, *values)
    return outs[:NY], outs[NY]


def attend_kernel(lens, token, q_ref, cache_ref, out_ref, token_out):
    rows, _, size, half = cache_ref.shape
    positions = 2 * half
    scale = size ** (-0.5)
    token_out[0] = token[0]
    chip, core, group = coordinates()
    first = (group * NC + core) * ROWS
    at = lax.broadcasted_iota(jnp.int32, (1, positions), 1)
    own = (chip * NC + core) * half
    other = (chip * NC + 1 - core) * half - half
    start = jnp.where(at < half, own, other)
    stats = [[], [], [], []]
    for j in range(rows):
        valid = at < lens[first + j] - start
        weights, pairs = [], []
        for k in range(2):
            lines = [slice(t * 32 + k * GROUP, t * 32 + (k + 1) * GROUP) for t in range(2)]
            q = jnp.concatenate([q_ref[j, part, :] for part in lines], 0)
            keys = jnp.concatenate([cache_ref[j, k], cache_ref[j, 2 + k]], 1)
            scores = jnp.dot(q, keys, preferred_element_type=F32) * scale
            scores = jnp.where(valid, scores, NEG_FILL)
            high, low = split_pair(jnp.max(scores, 1, keepdims=True))
            weight = jnp.where(valid, jnp.exp(scores - (high + low)), 0.0)
            pairs.append((high, low) + split_pair(jnp.sum(weight, 1, keepdims=True)))
            weights.append(weight.astype(BF16))
        values = jnp.concatenate(
            [
                jnp.concatenate([cache_ref[j, 4 + 2 * i], cache_ref[j, 5 + 2 * i]], 1)
                for i in range(2)
            ],
            0,
        )
        o = jnp.dot(jnp.concatenate(weights, 0), values, preferred_element_type=F32)
        for t in range(2):
            for k in range(2):
                line = t * 32 + k * GROUP
                part = o[k * 32 + t * GROUP : k * 32 + (t + 1) * GROUP, k * size : (k + 1) * size]
                out_ref[j, line : line + GROUP, :] = part.astype(BF16)
                for i in range(4):
                    stats[i].append(pairs[k][i][t * GROUP : (t + 1) * GROUP])
    stats = [jnp.concatenate(stat, 0) for stat in stats]
    lane = lax.broadcasted_iota(jnp.int32, (rows * LINES, 128), 1)
    table = jnp.where(lane == 0, stats[0], 0.0)
    for i in range(1, 4):
        table = jnp.where(lane == i, stats[i], table)
    table = table.T[:TAIL]
    for j in range(rows):
        tail = table[:, (j // 2) * 128 : (j // 2 + 1) * 128]
        if j % 2 == 1:
            tail = pltpu.roll(tail, LINES, 1)
        out_ref[j, LINES:, :] = tail.astype(BF16)


def attend(lens, token, queries, cache):
    rows, _, size, positions = cache.shape
    return pl.pallas_call(
        attend_kernel,
        in_specs=[SMEM] * 2 + [VMEM] * 2,
        out_specs=[VMEM, SMEM],
        out_shape=[
            jax.ShapeDtypeStruct((rows, BLOCK, size), BF16),
            jax.ShapeDtypeStruct((1,), jnp.int32),
        ],
        compiler_params=PARAMS,
        cost_estimate=pl.CostEstimate(
            flops=120 * ROWS * LINES * positions * size,
            bytes_accessed=160 * ROWS * positions * size,
            transcendentals=0,
        ),
    )(lens, token, queries, cache)


def to_owners_kernel(order, *refs):
    own, other, out_ref, slots = refs[:NY], refs[NY : 2 * NY], refs[2 * NY], refs[2 * NY + 1]
    _, core, y = coordinates()
    for slot in range(CHIPS * NC):
        slots[order[slot]] = slot
    for d in range(NY):
        group = lax.rem(y + d, NY)
        for c, source in ((core, own[d]), (1 - core, other[d])):
            for row in range(ROWS):
                slot = slots[(group * NC + c) * ROWS + row]

                @pl.when(lax.rem(slot, NC) == core)
                def _():
                    out_ref[slot // NC] = source[row]


def to_owners(order, own, other):
    return pl.pallas_call(
        to_owners_kernel,
        in_specs=[SMEM] + [VMEM] * (2 * NY),
        out_specs=VMEM,
        out_shape=jax.ShapeDtypeStruct((CHIPS,) + own[0].shape[1:], BF16),
        scratch_shapes=[pltpu.SMEM((CHIPS * NC,), jnp.int32)],
        compiler_params=PARAMS,
    )(order, *own, *other)


def finish_kernel(part_ref, q_ref, key_ref, value_ref, out_ref):
    size = q_ref.shape[1]
    scale = size ** (-0.5)
    tail = part_ref[:, LINES:, :].astype(F32)
    tops = tail[:, 0, :] + tail[:, 1, :]
    totals = tail[:, 2, :] + tail[:, 3, :]
    table = jnp.concatenate([tops, totals, jnp.zeros((128 - 2 * CHIPS, 128), F32)], 0).T[:LINES]
    tops, totals = table[:, :CHIPS], table[:, CHIPS : 2 * CHIPS]
    line = lax.broadcasted_iota(jnp.int32, (LINES, 1), 0)
    step = line // 32
    first = (line % 32) // GROUP == 0
    q = q_ref[...].astype(F32)
    top = jnp.max(tops, 1, keepdims=True)
    scores, values = [], []
    for u in range(2):
        pair = key_ref[u].astype(F32)
        key = jnp.where(first, pair[0:1], pair[1:2])
        pair = value_ref[u].astype(F32)
        values.append(jnp.where(first, pair[0:1], pair[1:2]))
        score = jnp.sum(q * key, -1, keepdims=True) * scale
        scores.append(jnp.where(u <= step, score, NEG_FILL))
        top = jnp.maximum(top, scores[u])
    factors = jnp.exp(tops - top)
    total = jnp.sum(factors * totals, 1, keepdims=True)
    accum = jnp.zeros((LINES, size), F32)
    for chip in range(CHIPS):
        accum = accum + factors[:, chip : chip + 1] * part_ref[chip, :LINES, :].astype(F32)
    for u in range(2):
        weight = jnp.where(u <= step, jnp.exp(scores[u] - top), 0.0)
        total = total + weight
        accum = accum + weight.astype(BF16).astype(F32) * values[u]
    out_ref[...] = (accum / total).astype(BF16)


def finish(parts, queries, new_keys, new_values):
    return pl.pallas_call(
        finish_kernel,
        in_specs=[VMEM] * 4,
        out_specs=VMEM,
        out_shape=jax.ShapeDtypeStruct(queries.shape, BF16),
        compiler_params=PARAMS,
    )(parts, queries, new_keys, new_values)


def over_chips(x):
    groups = [[chip * NC + c for chip in range(CHIPS)] for c in range(NC)]
    return lax.all_to_all(
        x, "seq", split_axis=0, concat_axis=0, axis_index_groups=groups, tiled=True
    )


def along_kvh(x, d):
    return lax.ppermute(x, "kvh", [(y, (y + d) % NY) for y in range(NY)])


def to_other_core(x):
    return lax.ppermute(x, "seq", [(i, i ^ 1) for i in range(CHIPS * NC)])


def on_device(queries, new_keys, new_values, cache_keys, cache_values, decode_order, cache_len):
    size = queries.shape[-1]

    other_keys, other_values = to_other_core(cache_keys), to_other_core(cache_values)

    own = queries.reshape(LINES, size)
    send, core = spread(own)
    got = over_chips(send)
    caches, token = by_head(core, (cache_keys, other_keys), (cache_values, other_values))
    passed, token = pass_on(token, got)
    sends = to_groups(decode_order, got, to_other_core(passed))

    parts = [None] * NY
    near = (1, 3, 2, 0)
    gots = {d: along_kvh(sends[d], d) if d else sends[d] for d in near}
    for d in near:
        part, token = attend(cache_len, token, gots[d], caches[d])
        parts[d] = along_kvh(part, NY - d) if d else part

    part = over_chips(to_owners(decode_order, parts, [to_other_core(part) for part in parts]))
    out = finish(part, own, new_keys[0], new_values[0])
    return out.reshape(queries.shape)


def solution(mesh):
    return jax.shard_map(
        on_device,
        mesh=mesh,
        in_specs=(
            P("seq", None, "kvh", None),
            P("seq", None, "kvh", None),
            P("seq", None, "kvh", None),
            P("kvh", "seq", None, None),
            P("kvh", "seq", None, None),
            P(),
            P(),
        ),
        out_specs=P("seq", None, "kvh", None),
        check_vma=False,
    )
```

```python
import jax
import jax.numpy as jnp
from jax import lax
from jax.experimental import pallas as pl
from jax.experimental.pallas import tpu as pltpu
from jax.sharding import PartitionSpec as P

NEG_FILL = -1e30
NC, NY = 2, 4
CHIPS = 32
GROUP = 16
ROWS = 8
HALF = 4
LINES = 64
TAIL = 8
BLOCK = LINES + TAIL
F32 = jnp.float32
BF16 = jnp.bfloat16
SMEM = pl.BlockSpec(memory_space=pltpu.SMEM)
VMEM = pl.BlockSpec(memory_space=pltpu.VMEM)
PARAMS = pltpu.CompilerParams(vmem_limit_bytes=16 * 2**20)
BRINGING = pl.CostEstimate(flops=2**30, bytes_accessed=2**24, transcendentals=0)


def split_pair(x):
    high = x.astype(BF16).astype(F32)
    low = (x - high).astype(BF16).astype(F32)
    return high, low


def coordinates():
    s = lax.axis_index("seq")
    return s // NC, lax.rem(s, NC), lax.axis_index("kvh")


def spread_kernel(own_ref, out_ref, core_ref):
    for chip in range(CHIPS):
        out_ref[chip] = own_ref[...]
    core_ref[0] = coordinates()[1]


def spread(own):
    return pl.pallas_call(
        spread_kernel,
        in_specs=[VMEM],
        out_specs=[VMEM, SMEM],
        out_shape=[
            jax.ShapeDtypeStruct((CHIPS,) + own.shape, BF16),
            jax.ShapeDtypeStruct((1,), jnp.int32),
        ],
        compiler_params=PARAMS,
    )(own)


def pass_on_kernel(token, got_ref, out_ref, token_out):
    out_ref[...] = got_ref[...]
    token_out[0] = token[0]


def pass_on(token, got):
    return pl.pallas_call(
        pass_on_kernel,
        in_specs=[SMEM, VMEM],
        out_specs=[VMEM, SMEM],
        out_shape=[
            jax.ShapeDtypeStruct(got.shape, got.dtype),
            jax.ShapeDtypeStruct((1,), jnp.int32),
        ],
        compiler_params=PARAMS,
        cost_estimate=BRINGING,
    )(token, got)


def to_groups_kernel(order, own_ref, other_ref, *refs):
    outs, slots = refs[:NY], refs[NY]
    _, core, y = coordinates()
    for slot in range(CHIPS * NC):
        slots[order[slot]] = slot
    for d in range(NY):
        group = lax.rem(y + d, NY)
        for row in range(ROWS):
            slot = slots[(group * NC + core) * ROWS + row]
            chip = slot // NC
            mine = lax.rem(slot, NC) == core
            outs[d][row] = jnp.where(mine, own_ref[chip], other_ref[chip])


def to_groups(order, own, other):
    _, lines, size = own.shape
    return pl.pallas_call(
        to_groups_kernel,
        in_specs=[SMEM, VMEM, VMEM],
        out_specs=[VMEM] * NY,
        out_shape=[jax.ShapeDtypeStruct((ROWS, lines, size), BF16)] * NY,
        scratch_shapes=[pltpu.SMEM((CHIPS * NC,), jnp.int32)],
        compiler_params=PARAMS,
        cost_estimate=BRINGING,
    )(order, own, other)


def by_head_kernel(core, *refs):
    ins, outs = refs[:4], refs[4 : 4 + NY]
    token, keep = refs[-2:]
    _, positions, kv, size = ins[0].shape
    y = coordinates()[2]
    token[0] = core[0]
    for slot in range(4):
        keep[slot] = ins[slot][0].reshape(positions * kv, size).astype(F32)
    for d in range(NY):
        quarter = lax.rem(y + NY - d, NY)
        for k in range(2):
            head = pl.ds(2 * quarter + k, positions, stride=kv)
            for i in range(2):
                outs[d][0, i * 2 + k] = keep[i, head, :].astype(BF16).T
                outs[d][0, 4 + i * 2 + k] = keep[2 + i, head, :].astype(BF16)


def by_head(core, keys, values):
    _, positions, kv, size = keys[0].shape
    rows = pl.BlockSpec((1, positions, kv, size), lambda i, core: (core[0] * ROWS + i, 0, 0, 0))
    tiles = (8, size, positions)
    outs = pl.pallas_call(
        by_head_kernel,
        grid_spec=pltpu.PrefetchScalarGridSpec(
            num_scalar_prefetch=1,
            grid=(ROWS,),
            in_specs=[rows] * 4,
            out_specs=[pl.BlockSpec((1,) + tiles, lambda i, core: (i, 0, 0, 0))] * NY + [SMEM],
            scratch_shapes=[pltpu.VMEM((4, positions * kv, size), F32)],
        ),
        out_shape=[jax.ShapeDtypeStruct((ROWS,) + tiles, BF16)] * NY
        + [jax.ShapeDtypeStruct((1,), jnp.int32)],
        cost_estimate=pl.CostEstimate(
            flops=0, bytes_accessed=16 * ROWS * positions * kv * size, transcendentals=0
        ),
    )(core, *keys, *values)
    return outs[:NY], outs[NY]


def attend_rows(base, lens, q_ref, cache_ref, out_ref):
    _, _, size, half = cache_ref.shape
    positions = 2 * half
    scale = size ** (-0.5)
    chip, core, group = coordinates()
    first = (group * NC + core) * ROWS + base
    at = lax.broadcasted_iota(jnp.int32, (1, positions), 1)
    own = (chip * NC + core) * half
    other = (chip * NC + 1 - core) * half - half
    start = jnp.where(at < half, own, other)
    stats = [[], [], [], []]
    for j in range(HALF):
        valid = at < lens[first + j] - start
        row = base + j
        weights, pairs = [], []
        for k in range(2):
            lines = [slice(t * 32 + k * GROUP, t * 32 + (k + 1) * GROUP) for t in range(2)]
            q = jnp.concatenate([q_ref[row, part, :] for part in lines], 0)
            keys = jnp.concatenate([cache_ref[row, k], cache_ref[row, 2 + k]], 1)
            scores = jnp.dot(q, keys, preferred_element_type=F32) * scale
            scores = jnp.where(valid, scores, NEG_FILL)
            high, low = split_pair(jnp.max(scores, 1, keepdims=True))
            weight = jnp.where(valid, jnp.exp(scores - (high + low)), 0.0)
            pairs.append((high, low) + split_pair(jnp.sum(weight, 1, keepdims=True)))
            weights.append(weight.astype(BF16))
        values = jnp.concatenate(
            [
                jnp.concatenate([cache_ref[row, 4 + 2 * i], cache_ref[row, 5 + 2 * i]], 1)
                for i in range(2)
            ],
            0,
        )
        o = jnp.dot(jnp.concatenate(weights, 0), values, preferred_element_type=F32)
        for t in range(2):
            for k in range(2):
                line = t * 32 + k * GROUP
                part = o[k * 32 + t * GROUP : k * 32 + (t + 1) * GROUP, k * size : (k + 1) * size]
                out_ref[row, line : line + GROUP, :] = part.astype(BF16)
                for i in range(4):
                    stats[i].append(pairs[k][i][t * GROUP : (t + 1) * GROUP])
    stats = [jnp.concatenate(stat, 0) for stat in stats]
    lane = lax.broadcasted_iota(jnp.int32, (HALF * LINES, 128), 1)
    table = jnp.where(lane == 0, stats[0], 0.0)
    for i in range(1, 4):
        table = jnp.where(lane == i, stats[i], table)
    table = table.T[:TAIL]
    for j in range(HALF):
        tail = table[:, (j // 2) * 128 : (j // 2 + 1) * 128]
        if j % 2 == 1:
            tail = pltpu.roll(tail, LINES, 1)
        out_ref[base + j, LINES:, :] = tail.astype(BF16)


def attend(lens, token, queries, cache, count=ROWS, done=None):
    rows, _, size, positions = cache.shape
    before = [] if done is None else [done]

    def kernel(lens, token, q_ref, cache_ref, *refs):
        out_ref, token_out = refs[-2:]
        token_out[0] = token[0]
        if before:
            out_ref[:HALF] = refs[0][...]
            attend_rows(HALF, lens, q_ref, cache_ref, out_ref)
        elif count == HALF:
            attend_rows(0, lens, q_ref, cache_ref, out_ref)
        else:

            def step(i, carry):
                attend_rows(i * HALF, lens, q_ref, cache_ref, out_ref)
                return carry

            lax.fori_loop(0, ROWS // HALF, step, 0)

    return pl.pallas_call(
        kernel,
        in_specs=[SMEM] * 2 + [VMEM] * (2 + len(before)),
        out_specs=[VMEM, SMEM],
        out_shape=[
            jax.ShapeDtypeStruct((count, BLOCK, size), BF16),
            jax.ShapeDtypeStruct((1,), jnp.int32),
        ],
        compiler_params=PARAMS,
        cost_estimate=pl.CostEstimate(
            flops=120 * ROWS * LINES * positions * size,
            bytes_accessed=160 * ROWS * positions * size,
            transcendentals=0,
        ),
    )(lens, token, queries, cache, *before)


def to_owners_kernel(order, *refs):
    own, other, out_ref, slots = refs[:NY], refs[NY : 2 * NY], refs[2 * NY], refs[2 * NY + 1]
    _, core, y = coordinates()
    for slot in range(CHIPS * NC):
        slots[order[slot]] = slot
    for d in range(NY):
        group = lax.rem(y + d, NY)
        for c, source in ((core, own[d]), (1 - core, other[d])):
            for row in range(ROWS):
                slot = slots[(group * NC + c) * ROWS + row]

                @pl.when(lax.rem(slot, NC) == core)
                def _():
                    out_ref[slot // NC] = source[row]


def to_owners(order, own, other):
    return pl.pallas_call(
        to_owners_kernel,
        in_specs=[SMEM] + [VMEM] * (2 * NY),
        out_specs=VMEM,
        out_shape=jax.ShapeDtypeStruct((CHIPS,) + own[0].shape[1:], BF16),
        scratch_shapes=[pltpu.SMEM((CHIPS * NC,), jnp.int32)],
        compiler_params=PARAMS,
    )(order, *own, *other)


def finish_kernel(part_ref, q_ref, key_ref, value_ref, out_ref):
    size = q_ref.shape[1]
    scale = size ** (-0.5)
    tail = part_ref[:, LINES:, :].astype(F32)
    tops = tail[:, 0, :] + tail[:, 1, :]
    totals = tail[:, 2, :] + tail[:, 3, :]
    table = jnp.concatenate([tops, totals, jnp.zeros((128 - 2 * CHIPS, 128), F32)], 0).T[:LINES]
    tops, totals = table[:, :CHIPS], table[:, CHIPS : 2 * CHIPS]
    line = lax.broadcasted_iota(jnp.int32, (LINES, 1), 0)
    step = line // 32
    first = (line % 32) // GROUP == 0
    q = q_ref[...].astype(F32)
    top = jnp.max(tops, 1, keepdims=True)
    scores, values = [], []
    for u in range(2):
        pair = key_ref[u].astype(F32)
        key = jnp.where(first, pair[0:1], pair[1:2])
        pair = value_ref[u].astype(F32)
        values.append(jnp.where(first, pair[0:1], pair[1:2]))
        score = jnp.sum(q * key, -1, keepdims=True) * scale
        scores.append(jnp.where(u <= step, score, NEG_FILL))
        top = jnp.maximum(top, scores[u])
    factors = jnp.exp(tops - top)
    total = jnp.sum(factors * totals, 1, keepdims=True)
    accum = jnp.zeros((LINES, size), F32)
    for chip in range(CHIPS):
        accum = accum + factors[:, chip : chip + 1] * part_ref[chip, :LINES, :].astype(F32)
    for u in range(2):
        weight = jnp.where(u <= step, jnp.exp(scores[u] - top), 0.0)
        total = total + weight
        accum = accum + weight.astype(BF16).astype(F32) * values[u]
    out_ref[...] = (accum / total).astype(BF16)


def finish(parts, queries, new_keys, new_values):
    return pl.pallas_call(
        finish_kernel,
        in_specs=[VMEM] * 4,
        out_specs=VMEM,
        out_shape=jax.ShapeDtypeStruct(queries.shape, BF16),
        compiler_params=PARAMS,
    )(parts, queries, new_keys, new_values)


def over_chips(x):
    groups = [[chip * NC + c for chip in range(CHIPS)] for c in range(NC)]
    return lax.all_to_all(
        x, "seq", split_axis=0, concat_axis=0, axis_index_groups=groups, tiled=True
    )


def along_kvh(x, d):
    return lax.ppermute(x, "kvh", [(y, (y + d) % NY) for y in range(NY)])


def to_other_core(x):
    return lax.ppermute(x, "seq", [(i, i ^ 1) for i in range(CHIPS * NC)])


def on_device(queries, new_keys, new_values, cache_keys, cache_values, decode_order, cache_len):
    size = queries.shape[-1]

    other_keys, other_values = to_other_core(cache_keys), to_other_core(cache_values)

    own = queries.reshape(LINES, size)
    send, core = spread(own)
    got = over_chips(send)
    caches, token = by_head(core, (cache_keys, other_keys), (cache_values, other_values))
    passed, token = pass_on(token, got)
    sends = to_groups(decode_order, got, to_other_core(passed))

    gots = {d: along_kvh(sends[d], d) for d in (1, 3, 2)}
    half, token = attend(cache_len, token, sends[0], caches[0], count=HALF)
    parts = [None] * NY
    for d in (1, 3, 2):
        part, _ = attend(cache_len, token, gots[d], caches[d])
        parts[d] = along_kvh(part, NY - d)
    parts[0], _ = attend(cache_len, token, sends[0], caches[0], done=half)

    part = over_chips(to_owners(decode_order, parts, [to_other_core(part) for part in parts]))
    out = finish(part, own, new_keys[0], new_values[0])
    return out.reshape(queries.shape)


def solution(mesh):
    return jax.shard_map(
        on_device,
        mesh=mesh,
        in_specs=(
            P("seq", None, "kvh", None),
            P("seq", None, "kvh", None),
            P("seq", None, "kvh", None),
            P("kvh", "seq", None, None),
            P("kvh", "seq", None, None),
            P(),
            P(),
        ),
        out_specs=P("seq", None, "kvh", None),
        check_vma=False,
    )
```

```python
import jax
import jax.numpy as jnp
from jax import lax
from jax.experimental import pallas as pl
from jax.experimental.pallas import tpu as pltpu
from jax.sharding import PartitionSpec as P

NEG_FILL = -1e30
NC, NY = 2, 4
CHIPS = 32
GROUP = 16
ROWS = 8
LINES = 64
TAIL = 8
BLOCK = LINES + TAIL
F32 = jnp.float32
BF16 = jnp.bfloat16
SMEM = pl.BlockSpec(memory_space=pltpu.SMEM)
VMEM = pl.BlockSpec(memory_space=pltpu.VMEM)
PARAMS = pltpu.CompilerParams(vmem_limit_bytes=16 * 2**20)
BRINGING = pl.CostEstimate(flops=2**30, bytes_accessed=2**24, transcendentals=0)


def split_pair(x):
    high = x.astype(BF16).astype(F32)
    low = (x - high).astype(BF16).astype(F32)
    return high, low


def coordinates():
    s = lax.axis_index("seq")
    return s // NC, lax.rem(s, NC), lax.axis_index("kvh")


def spread_kernel(own_ref, out_ref, core_ref):
    for chip in range(CHIPS):
        out_ref[chip] = own_ref[...]
    core_ref[0] = coordinates()[1]


def spread(own):
    return pl.pallas_call(
        spread_kernel,
        in_specs=[VMEM],
        out_specs=[VMEM, SMEM],
        out_shape=[
            jax.ShapeDtypeStruct((CHIPS,) + own.shape, BF16),
            jax.ShapeDtypeStruct((1,), jnp.int32),
        ],
        compiler_params=PARAMS,
    )(own)


def pass_on_kernel(token, got_ref, out_ref):
    out_ref[...] = got_ref[...]


def pass_on(token, got):
    return pl.pallas_call(
        pass_on_kernel,
        in_specs=[SMEM, VMEM],
        out_specs=VMEM,
        out_shape=jax.ShapeDtypeStruct(got.shape, got.dtype),
        compiler_params=PARAMS,
        cost_estimate=BRINGING,
    )(token, got)


def to_groups_kernel(order, own_ref, other_ref, *refs):
    outs, slots = refs[:NY], refs[NY]
    _, core, y = coordinates()
    for slot in range(CHIPS * NC):
        slots[order[slot]] = slot
    for d in range(NY):
        group = lax.rem(y + d, NY)
        for row in range(ROWS):
            slot = slots[(group * NC + core) * ROWS + row]
            chip = slot // NC
            mine = lax.rem(slot, NC) == core
            outs[d][row] = jnp.where(mine, own_ref[chip], other_ref[chip])


def to_groups(order, own, other):
    _, lines, size = own.shape
    return pl.pallas_call(
        to_groups_kernel,
        in_specs=[SMEM, VMEM, VMEM],
        out_specs=[VMEM] * NY,
        out_shape=[jax.ShapeDtypeStruct((ROWS, lines, size), BF16)] * NY,
        scratch_shapes=[pltpu.SMEM((CHIPS * NC,), jnp.int32)],
        compiler_params=PARAMS,
        cost_estimate=BRINGING,
    )(order, own, other)


def by_head_kernel(core, *refs):
    ins, outs = refs[:4], refs[4 : 4 + NY]
    token, keep = refs[-2:]
    _, positions, kv, size = ins[0].shape
    y = coordinates()[2]
    token[0] = core[0]
    for slot in range(4):
        keep[slot] = ins[slot][0].reshape(positions * kv, size).astype(F32)
    for d in range(NY):
        quarter = lax.rem(y + NY - d, NY)
        for k in range(2):
            head = pl.ds(2 * quarter + k, positions, stride=kv)
            for i in range(2):
                outs[d][0, i * 2 + k] = keep[i, head, :].astype(BF16).T
                outs[d][0, 4 + i * 2 + k] = keep[2 + i, head, :].astype(BF16)


def by_head(core, keys, values):
    _, positions, kv, size = keys[0].shape
    rows = pl.BlockSpec((1, positions, kv, size), lambda i, core: (core[0] * ROWS + i, 0, 0, 0))
    tiles = (8, size, positions)
    outs = pl.pallas_call(
        by_head_kernel,
        grid_spec=pltpu.PrefetchScalarGridSpec(
            num_scalar_prefetch=1,
            grid=(ROWS,),
            in_specs=[rows] * 4,
            out_specs=[pl.BlockSpec((1,) + tiles, lambda i, core: (i, 0, 0, 0))] * NY + [SMEM],
            scratch_shapes=[pltpu.VMEM((4, positions * kv, size), F32)],
        ),
        out_shape=[jax.ShapeDtypeStruct((ROWS,) + tiles, BF16)] * NY
        + [jax.ShapeDtypeStruct((1,), jnp.int32)],
        cost_estimate=pl.CostEstimate(
            flops=0, bytes_accessed=16 * ROWS * positions * kv * size, transcendentals=0
        ),
    )(core, *keys, *values)
    return outs[:NY], outs[NY]


def attend_kernel(lens, q_ref, cache_ref, out_ref):
    rows, _, size, half = cache_ref.shape
    positions = 2 * half
    scale = size ** (-0.5)
    chip, core, group = coordinates()
    first = (group * NC + core) * ROWS
    at = lax.broadcasted_iota(jnp.int32, (1, positions), 1)
    own = (chip * NC + core) * half
    other = (chip * NC + 1 - core) * half - half
    start = jnp.where(at < half, own, other)
    base = jnp.minimum(lens[first], 0)
    stats = [[], [], [], []]
    for j in range(rows):
        valid = at < lens[first + j] - start
        weights, pairs = [], []
        for k in range(2):
            lines = [slice(t * 32 + k * GROUP, t * 32 + (k + 1) * GROUP) for t in range(2)]
            q = jnp.concatenate([q_ref[j, part, :] for part in lines], 0)
            keys = jnp.concatenate([cache_ref[j, base + k], cache_ref[j, base + 2 + k]], 1)
            scores = jnp.dot(q, keys, preferred_element_type=F32) * scale
            scores = jnp.where(valid, scores, NEG_FILL)
            high, low = split_pair(jnp.max(scores, 1, keepdims=True))
            weight = jnp.where(valid, jnp.exp(scores - (high + low)), 0.0)
            pairs.append((high, low) + split_pair(jnp.sum(weight, 1, keepdims=True)))
            weights.append(weight.astype(BF16))
        values = jnp.concatenate(
            [
                jnp.concatenate([cache_ref[j, base + 4 + 2 * i], cache_ref[j, base + 5 + 2 * i]], 1)
                for i in range(2)
            ],
            0,
        )
        o = jnp.dot(jnp.concatenate(weights, 0), values, preferred_element_type=F32)
        for t in range(2):
            for k in range(2):
                line = t * 32 + k * GROUP
                part = o[k * 32 + t * GROUP : k * 32 + (t + 1) * GROUP, k * size : (k + 1) * size]
                out_ref[j, line : line + GROUP, :] = part.astype(BF16)
                for i in range(4):
                    stats[i].append(pairs[k][i][t * GROUP : (t + 1) * GROUP])
    stats = [jnp.concatenate(stat, 0) for stat in stats]
    lane = lax.broadcasted_iota(jnp.int32, (rows * LINES, 128), 1)
    table = jnp.where(lane == 0, stats[0], 0.0)
    for i in range(1, 4):
        table = jnp.where(lane == i, stats[i], table)
    table = table.T[:TAIL]
    for j in range(rows):
        tail = table[:, (j // 2) * 128 : (j // 2 + 1) * 128]
        if j % 2 == 1:
            tail = pltpu.roll(tail, LINES, 1)
        out_ref[j, LINES:, :] = tail.astype(BF16)


def attend(lens, queries, cache):
    rows, _, size, positions = cache.shape
    return pl.pallas_call(
        attend_kernel,
        in_specs=[SMEM, VMEM, VMEM],
        out_specs=VMEM,
        out_shape=jax.ShapeDtypeStruct((rows, BLOCK, size), BF16),
        compiler_params=PARAMS,
        cost_estimate=pl.CostEstimate(
            flops=120 * ROWS * LINES * positions * size,
            bytes_accessed=160 * ROWS * positions * size,
            transcendentals=0,
        ),
    )(lens, queries, cache)


def to_owners_kernel(order, *refs):
    own, other, out_ref, slots = refs[:NY], refs[NY : 2 * NY], refs[2 * NY], refs[2 * NY + 1]
    _, core, y = coordinates()
    for slot in range(CHIPS * NC):
        slots[order[slot]] = slot
    for d in range(NY):
        group = lax.rem(y + d, NY)
        for c, source in ((core, own[d]), (1 - core, other[d])):
            for row in range(ROWS):
                slot = slots[(group * NC + c) * ROWS + row]

                @pl.when(lax.rem(slot, NC) == core)
                def _():
                    out_ref[slot // NC] = source[row]


def to_owners(order, own, other):
    return pl.pallas_call(
        to_owners_kernel,
        in_specs=[SMEM] + [VMEM] * (2 * NY),
        out_specs=VMEM,
        out_shape=jax.ShapeDtypeStruct((CHIPS,) + own[0].shape[1:], BF16),
        scratch_shapes=[pltpu.SMEM((CHIPS * NC,), jnp.int32)],
        compiler_params=PARAMS,
    )(order, *own, *other)


def finish_kernel(part_ref, q_ref, key_ref, value_ref, out_ref):
    size = q_ref.shape[1]
    scale = size ** (-0.5)
    tail = part_ref[:, LINES:, :].astype(F32)
    tops = tail[:, 0, :] + tail[:, 1, :]
    totals = tail[:, 2, :] + tail[:, 3, :]
    table = jnp.concatenate([tops, totals, jnp.zeros((128 - 2 * CHIPS, 128), F32)], 0).T[:LINES]
    tops, totals = table[:, :CHIPS], table[:, CHIPS : 2 * CHIPS]
    line = lax.broadcasted_iota(jnp.int32, (LINES, 1), 0)
    step = line // 32
    first = (line % 32) // GROUP == 0
    q = q_ref[...].astype(F32)
    top = jnp.max(tops, 1, keepdims=True)
    scores, values = [], []
    for u in range(2):
        pair = key_ref[u].astype(F32)
        key = jnp.where(first, pair[0:1], pair[1:2])
        pair = value_ref[u].astype(F32)
        values.append(jnp.where(first, pair[0:1], pair[1:2]))
        score = jnp.sum(q * key, -1, keepdims=True) * scale
        scores.append(jnp.where(u <= step, score, NEG_FILL))
        top = jnp.maximum(top, scores[u])
    factors = jnp.exp(tops - top)
    total = jnp.sum(factors * totals, 1, keepdims=True)
    accum = jnp.zeros((LINES, size), F32)
    for chip in range(CHIPS):
        accum = accum + factors[:, chip : chip + 1] * part_ref[chip, :LINES, :].astype(F32)
    for u in range(2):
        weight = jnp.where(u <= step, jnp.exp(scores[u] - top), 0.0)
        total = total + weight
        accum = accum + weight.astype(BF16).astype(F32) * values[u]
    out_ref[...] = (accum / total).astype(BF16)


def finish(parts, queries, new_keys, new_values):
    return pl.pallas_call(
        finish_kernel,
        in_specs=[VMEM] * 4,
        out_specs=VMEM,
        out_shape=jax.ShapeDtypeStruct(queries.shape, BF16),
        compiler_params=PARAMS,
    )(parts, queries, new_keys, new_values)


def over_chips(x):
    groups = [[chip * NC + c for chip in range(CHIPS)] for c in range(NC)]
    return lax.all_to_all(
        x, "seq", split_axis=0, concat_axis=0, axis_index_groups=groups, tiled=True
    )


def along_kvh(x, d):
    return lax.ppermute(x, "kvh", [(y, (y + d) % NY) for y in range(NY)])


def to_other_core(x):
    return lax.ppermute(x, "seq", [(i, i ^ 1) for i in range(CHIPS * NC)])


def on_device(queries, new_keys, new_values, cache_keys, cache_values, decode_order, cache_len):
    size = queries.shape[-1]

    other_keys, other_values = to_other_core(cache_keys), to_other_core(cache_values)

    own = queries.reshape(LINES, size)
    send, core = spread(own)
    got = over_chips(send)
    caches, token = by_head(core, (cache_keys, other_keys), (cache_values, other_values))
    sends = to_groups(decode_order, got, to_other_core(pass_on(token, got)))

    parts = [None] * NY
    for d in range(NY):
        queries_d = along_kvh(sends[d], d) if d else sends[d]
        part = attend(cache_len, queries_d, caches[d])
        parts[d] = along_kvh(part, NY - d) if d else part

    part = over_chips(to_owners(decode_order, parts, [to_other_core(part) for part in parts]))
    out = finish(part, own, new_keys[0], new_values[0])
    return out.reshape(queries.shape)


def solution(mesh):
    return jax.shard_map(
        on_device,
        mesh=mesh,
        in_specs=(
            P("seq", None, "kvh", None),
            P("seq", None, "kvh", None),
            P("seq", None, "kvh", None),
            P("kvh", "seq", None, None),
            P("kvh", "seq", None, None),
            P(),
            P(),
        ),
        out_specs=P("seq", None, "kvh", None),
        check_vma=False,
    )
```

```python
import jax
import jax.numpy as jnp
from jax import lax
from jax.experimental import pallas as pl
from jax.experimental.pallas import tpu as pltpu
from jax.sharding import PartitionSpec as P

NEG_FILL = -1e30
NC, NY = 2, 4
CHIPS = 32
GROUP = 16
ROWS = 8
LINES = 64
TAIL = 8
BLOCK = LINES + TAIL
F32 = jnp.float32
BF16 = jnp.bfloat16
SMEM = pl.BlockSpec(memory_space=pltpu.SMEM)
VMEM = pl.BlockSpec(memory_space=pltpu.VMEM)
PARAMS = pltpu.CompilerParams(vmem_limit_bytes=16 * 2**20)
BRINGING = pl.CostEstimate(flops=2**30, bytes_accessed=2**24, transcendentals=0)


def split_pair(x):
    high = x.astype(BF16).astype(F32)
    low = (x - high).astype(BF16).astype(F32)
    return high, low


def coordinates():
    s = lax.axis_index("seq")
    return s // NC, lax.rem(s, NC), lax.axis_index("kvh")


def spread_kernel(own_ref, out_ref, core_ref):
    for chip in range(CHIPS):
        out_ref[chip] = own_ref[...]
    core_ref[0] = coordinates()[1]


def spread(own):
    return pl.pallas_call(
        spread_kernel,
        in_specs=[VMEM],
        out_specs=[VMEM, SMEM],
        out_shape=[
            jax.ShapeDtypeStruct((CHIPS,) + own.shape, BF16),
            jax.ShapeDtypeStruct((1,), jnp.int32),
        ],
        compiler_params=PARAMS,
    )(own)


def pass_on_kernel(token, got_ref, out_ref):
    out_ref[...] = got_ref[...]


def pass_on(token, got):
    return pl.pallas_call(
        pass_on_kernel,
        in_specs=[SMEM, VMEM],
        out_specs=VMEM,
        out_shape=jax.ShapeDtypeStruct(got.shape, got.dtype),
        compiler_params=PARAMS,
        cost_estimate=BRINGING,
    )(token, got)


def to_groups_kernel(order, own_ref, other_ref, *refs):
    outs, slots = refs[:NY], refs[NY]
    _, core, y = coordinates()
    for slot in range(CHIPS * NC):
        slots[order[slot]] = slot
    for d in range(NY):
        group = lax.rem(y + d, NY)
        for row in range(ROWS):
            slot = slots[(group * NC + core) * ROWS + row]
            chip = slot // NC
            mine = lax.rem(slot, NC) == core
            outs[d][row] = jnp.where(mine, own_ref[chip], other_ref[chip])


def to_groups(order, own, other):
    _, lines, size = own.shape
    return pl.pallas_call(
        to_groups_kernel,
        in_specs=[SMEM, VMEM, VMEM],
        out_specs=[VMEM] * NY,
        out_shape=[jax.ShapeDtypeStruct((ROWS, lines, size), BF16)] * NY,
        scratch_shapes=[pltpu.SMEM((CHIPS * NC,), jnp.int32)],
        compiler_params=PARAMS,
        cost_estimate=BRINGING,
    )(order, own, other)


def by_head_kernel(core, *refs):
    ins, outs = refs[:4], refs[4 : 4 + NY]
    token, keep = refs[-2:]
    _, positions, kv, size = ins[0].shape
    y = coordinates()[2]
    token[0] = core[0]
    for slot in range(4):
        keep[slot] = ins[slot][0].reshape(positions * kv, size).astype(F32)
    for d in range(NY):
        quarter = lax.rem(y + NY - d, NY)
        for k in range(2):
            head = pl.ds(2 * quarter + k, positions, stride=kv)
            for i in range(2):
                outs[d][0, i * 2 + k] = keep[i, head, :].astype(BF16).T
                outs[d][0, 4 + i * 2 + k] = keep[2 + i, head, :].astype(BF16)


def by_head(core, keys, values):
    _, positions, kv, size = keys[0].shape
    rows = pl.BlockSpec((1, positions, kv, size), lambda i, core: (core[0] * ROWS + i, 0, 0, 0))
    tiles = (8, size, positions)
    outs = pl.pallas_call(
        by_head_kernel,
        grid_spec=pltpu.PrefetchScalarGridSpec(
            num_scalar_prefetch=1,
            grid=(ROWS,),
            in_specs=[rows] * 4,
            out_specs=[pl.BlockSpec((1,) + tiles, lambda i, core: (i, 0, 0, 0))] * NY + [SMEM],
            scratch_shapes=[pltpu.VMEM((4, positions * kv, size), F32)],
        ),
        out_shape=[jax.ShapeDtypeStruct((ROWS,) + tiles, BF16)] * NY
        + [jax.ShapeDtypeStruct((1,), jnp.int32)],
        cost_estimate=pl.CostEstimate(
            flops=0, bytes_accessed=16 * ROWS * positions * kv * size, transcendentals=0
        ),
    )(core, *keys, *values)
    return outs[:NY], outs[NY]


def attend_kernel(lens, q_ref, cache_ref, *refs):
    out_ref, token = refs[-2:]
    rows, _, size, half = cache_ref.shape
    positions = 2 * half
    scale = size ** (-0.5)
    chip, core, group = coordinates()
    first = (group * NC + core) * ROWS
    at = lax.broadcasted_iota(jnp.int32, (1, positions), 1)
    own = (chip * NC + core) * half
    other = (chip * NC + 1 - core) * half - half
    start = jnp.where(at < half, own, other)
    base = jnp.minimum(lens[first], 0)
    token[0] = base
    stats = [[], [], [], []]
    for j in range(rows):
        valid = at < lens[first + j] - start
        weights, pairs = [], []
        for k in range(2):
            lines = [slice(t * 32 + k * GROUP, t * 32 + (k + 1) * GROUP) for t in range(2)]
            q = jnp.concatenate([q_ref[j, part, :] for part in lines], 0)
            keys = jnp.concatenate([cache_ref[j, base + k], cache_ref[j, base + 2 + k]], 1)
            scores = jnp.dot(q, keys, preferred_element_type=F32) * scale
            scores = jnp.where(valid, scores, NEG_FILL)
            high, low = split_pair(jnp.max(scores, 1, keepdims=True))
            weight = jnp.where(valid, jnp.exp(scores - (high + low)), 0.0)
            pairs.append((high, low) + split_pair(jnp.sum(weight, 1, keepdims=True)))
            weights.append(weight.astype(BF16))
        values = jnp.concatenate(
            [
                jnp.concatenate([cache_ref[j, base + 4 + 2 * i], cache_ref[j, base + 5 + 2 * i]], 1)
                for i in range(2)
            ],
            0,
        )
        o = jnp.dot(jnp.concatenate(weights, 0), values, preferred_element_type=F32)
        for t in range(2):
            for k in range(2):
                line = t * 32 + k * GROUP
                part = o[k * 32 + t * GROUP : k * 32 + (t + 1) * GROUP, k * size : (k + 1) * size]
                out_ref[j, line : line + GROUP, :] = part.astype(BF16)
                for i in range(4):
                    stats[i].append(pairs[k][i][t * GROUP : (t + 1) * GROUP])
    stats = [jnp.concatenate(stat, 0) for stat in stats]
    lane = lax.broadcasted_iota(jnp.int32, (rows * LINES, 128), 1)
    table = jnp.where(lane == 0, stats[0], 0.0)
    for i in range(1, 4):
        table = jnp.where(lane == i, stats[i], table)
    table = table.T[:TAIL]
    for j in range(rows):
        tail = table[:, (j // 2) * 128 : (j // 2 + 1) * 128]
        if j % 2 == 1:
            tail = pltpu.roll(tail, LINES, 1)
        out_ref[j, LINES:, :] = tail.astype(BF16)


def attend(lens, queries, cache, before):
    rows, _, size, positions = cache.shape
    return pl.pallas_call(
        attend_kernel,
        in_specs=[SMEM, VMEM, VMEM] + [SMEM] * len(before),
        out_specs=[VMEM, SMEM],
        out_shape=[
            jax.ShapeDtypeStruct((rows, BLOCK, size), BF16),
            jax.ShapeDtypeStruct((1,), jnp.int32),
        ],
        compiler_params=PARAMS,
        cost_estimate=pl.CostEstimate(
            flops=120 * ROWS * LINES * positions * size,
            bytes_accessed=160 * ROWS * positions * size,
            transcendentals=0,
        ),
    )(lens, queries, cache, *before)


def to_owners_kernel(order, *refs):
    own, other, out_ref, slots = refs[:NY], refs[NY : 2 * NY], refs[2 * NY], refs[2 * NY + 1]
    _, core, y = coordinates()
    for slot in range(CHIPS * NC):
        slots[order[slot]] = slot
    for d in range(NY):
        group = lax.rem(y + d, NY)
        for c, source in ((core, own[d]), (1 - core, other[d])):
            for row in range(ROWS):
                slot = slots[(group * NC + c) * ROWS + row]

                @pl.when(lax.rem(slot, NC) == core)
                def _():
                    out_ref[slot // NC] = source[row]


def to_owners(order, own, other):
    return pl.pallas_call(
        to_owners_kernel,
        in_specs=[SMEM] + [VMEM] * (2 * NY),
        out_specs=VMEM,
        out_shape=jax.ShapeDtypeStruct((CHIPS,) + own[0].shape[1:], BF16),
        scratch_shapes=[pltpu.SMEM((CHIPS * NC,), jnp.int32)],
        compiler_params=PARAMS,
    )(order, *own, *other)


def finish_kernel(part_ref, q_ref, key_ref, value_ref, out_ref):
    size = q_ref.shape[1]
    scale = size ** (-0.5)
    tail = part_ref[:, LINES:, :].astype(F32)
    tops = tail[:, 0, :] + tail[:, 1, :]
    totals = tail[:, 2, :] + tail[:, 3, :]
    table = jnp.concatenate([tops, totals, jnp.zeros((128 - 2 * CHIPS, 128), F32)], 0).T[:LINES]
    tops, totals = table[:, :CHIPS], table[:, CHIPS : 2 * CHIPS]
    line = lax.broadcasted_iota(jnp.int32, (LINES, 1), 0)
    step = line // 32
    first = (line % 32) // GROUP == 0
    q = q_ref[...].astype(F32)
    top = jnp.max(tops, 1, keepdims=True)
    scores, values = [], []
    for u in range(2):
        pair = key_ref[u].astype(F32)
        key = jnp.where(first, pair[0:1], pair[1:2])
        pair = value_ref[u].astype(F32)
        values.append(jnp.where(first, pair[0:1], pair[1:2]))
        score = jnp.sum(q * key, -1, keepdims=True) * scale
        scores.append(jnp.where(u <= step, score, NEG_FILL))
        top = jnp.maximum(top, scores[u])
    factors = jnp.exp(tops - top)
    total = jnp.sum(factors * totals, 1, keepdims=True)
    accum = jnp.zeros((LINES, size), F32)
    for chip in range(CHIPS):
        accum = accum + factors[:, chip : chip + 1] * part_ref[chip, :LINES, :].astype(F32)
    for u in range(2):
        weight = jnp.where(u <= step, jnp.exp(scores[u] - top), 0.0)
        total = total + weight
        accum = accum + weight.astype(BF16).astype(F32) * values[u]
    out_ref[...] = (accum / total).astype(BF16)


def finish(parts, queries, new_keys, new_values):
    return pl.pallas_call(
        finish_kernel,
        in_specs=[VMEM] * 4,
        out_specs=VMEM,
        out_shape=jax.ShapeDtypeStruct(queries.shape, BF16),
        compiler_params=PARAMS,
    )(parts, queries, new_keys, new_values)


def over_chips(x):
    groups = [[chip * NC + c for chip in range(CHIPS)] for c in range(NC)]
    return lax.all_to_all(
        x, "seq", split_axis=0, concat_axis=0, axis_index_groups=groups, tiled=True
    )


def along_kvh(x, d):
    return lax.ppermute(x, "kvh", [(y, (y + d) % NY) for y in range(NY)])


def to_other_core(x):
    return lax.ppermute(x, "seq", [(i, i ^ 1) for i in range(CHIPS * NC)])


def on_device(queries, new_keys, new_values, cache_keys, cache_values, decode_order, cache_len):
    size = queries.shape[-1]

    other_keys, other_values = to_other_core(cache_keys), to_other_core(cache_values)

    own = queries.reshape(LINES, size)
    send, core = spread(own)
    got = over_chips(send)
    caches, token = by_head(core, (cache_keys, other_keys), (cache_values, other_values))
    sends = to_groups(decode_order, got, to_other_core(pass_on(token, got)))

    parts = [None] * NY
    near = (1, 3, 2, 0)
    gots = {d: along_kvh(sends[d], d) if d else sends[d] for d in near}
    before = ()
    for d in near:
        part, *before = attend(cache_len, gots[d], caches[d], before)
        parts[d] = along_kvh(part, NY - d) if d else part

    part = over_chips(to_owners(decode_order, parts, [to_other_core(part) for part in parts]))
    out = finish(part, own, new_keys[0], new_values[0])
    return out.reshape(queries.shape)


def solution(mesh):
    return jax.shard_map(
        on_device,
        mesh=mesh,
        in_specs=(
            P("seq", None, "kvh", None),
            P("seq", None, "kvh", None),
            P("seq", None, "kvh", None),
            P("kvh", "seq", None, None),
            P("kvh", "seq", None, None),
            P(),
            P(),
        ),
        out_specs=P("seq", None, "kvh", None),
        check_vma=False,
    )
```

```python
import jax
import jax.numpy as jnp
from jax import lax
from jax.experimental import pallas as pl
from jax.experimental.pallas import tpu as pltpu
from jax.sharding import PartitionSpec as P

NEG_FILL = -1e30
NC, NY = 2, 4
CHIPS = 32
GROUP = 16
ROWS = 8
LINES = 64
TAIL = 8
BLOCK = LINES + TAIL
F32 = jnp.float32
BF16 = jnp.bfloat16
SMEM = pl.BlockSpec(memory_space=pltpu.SMEM)
VMEM = pl.BlockSpec(memory_space=pltpu.VMEM)
ANY = pl.BlockSpec(memory_space=pl.ANY)
PARAMS = pltpu.CompilerParams(vmem_limit_bytes=16 * 2**20)
BRINGING = pl.CostEstimate(flops=2**30, bytes_accessed=2**24, transcendentals=0)


def split_pair(x):
    high = x.astype(BF16).astype(F32)
    low = (x - high).astype(BF16).astype(F32)
    return high, low


def coordinates():
    s = lax.axis_index("seq")
    return s // NC, lax.rem(s, NC), lax.axis_index("kvh")


def spread_kernel(own_ref, out_ref, core_ref):
    for chip in range(CHIPS):
        out_ref[chip] = own_ref[...]
    core_ref[0] = coordinates()[1]


def spread(own):
    return pl.pallas_call(
        spread_kernel,
        in_specs=[VMEM],
        out_specs=[VMEM, SMEM],
        out_shape=[
            jax.ShapeDtypeStruct((CHIPS,) + own.shape, BF16),
            jax.ShapeDtypeStruct((1,), jnp.int32),
        ],
        compiler_params=PARAMS,
    )(own)


def pass_on_kernel(token, got_ref, out_ref):
    out_ref[...] = got_ref[...]


def pass_on(token, got):
    return pl.pallas_call(
        pass_on_kernel,
        in_specs=[SMEM, VMEM],
        out_specs=VMEM,
        out_shape=jax.ShapeDtypeStruct(got.shape, got.dtype),
        compiler_params=PARAMS,
        cost_estimate=BRINGING,
    )(token, got)


def to_groups_kernel(order, own_ref, other_ref, *refs):
    outs, slots = refs[:NY], refs[NY]
    _, core, y = coordinates()
    for slot in range(CHIPS * NC):
        slots[order[slot]] = slot
    for d in range(NY):
        group = lax.rem(y + d, NY)
        for row in range(ROWS):
            slot = slots[(group * NC + core) * ROWS + row]
            chip = slot // NC
            mine = lax.rem(slot, NC) == core
            outs[d][row] = jnp.where(mine, own_ref[chip], other_ref[chip])


def to_groups(order, own, other):
    _, lines, size = own.shape
    return pl.pallas_call(
        to_groups_kernel,
        in_specs=[SMEM, VMEM, VMEM],
        out_specs=[VMEM] * NY,
        out_shape=[jax.ShapeDtypeStruct((ROWS, lines, size), BF16)] * NY,
        scratch_shapes=[pltpu.SMEM((CHIPS * NC,), jnp.int32)],
        compiler_params=PARAMS,
        cost_estimate=BRINGING,
    )(order, own, other)


def by_head_kernel(core, *refs):
    ins, outs = refs[:4], refs[4 : 4 + NY]
    token, keep = refs[-2:]
    _, positions, kv, size = ins[0].shape
    y = coordinates()[2]
    token[0] = core[0]
    for slot in range(4):
        keep[slot] = ins[slot][0].reshape(positions * kv, size).astype(F32)
    for d in range(NY):
        quarter = lax.rem(y + NY - d, NY)
        for k in range(2):
            head = pl.ds(2 * quarter + k, positions, stride=kv)
            for i in range(2):
                outs[d][0, i * 2 + k] = keep[i, head, :].astype(BF16).T
                outs[d][0, 4 + i * 2 + k] = keep[2 + i, head, :].astype(BF16)


def by_head(core, keys, values):
    _, positions, kv, size = keys[0].shape
    rows = pl.BlockSpec((1, positions, kv, size), lambda i, core: (core[0] * ROWS + i, 0, 0, 0))
    tiles = (8, size, positions)
    outs = pl.pallas_call(
        by_head_kernel,
        grid_spec=pltpu.PrefetchScalarGridSpec(
            num_scalar_prefetch=1,
            grid=(ROWS,),
            in_specs=[rows] * 4,
            out_specs=[pl.BlockSpec((1,) + tiles, lambda i, core: (i, 0, 0, 0))] * NY + [SMEM],
            scratch_shapes=[pltpu.VMEM((4, positions * kv, size), F32)],
        ),
        out_shape=[jax.ShapeDtypeStruct((ROWS,) + tiles, BF16)] * NY
        + [jax.ShapeDtypeStruct((1,), jnp.int32)],
        cost_estimate=pl.CostEstimate(
            flops=0, bytes_accessed=16 * ROWS * positions * kv * size, transcendentals=0
        ),
    )(core, *keys, *values)
    return outs[:NY], outs[NY]


def attend_kernel(lens, q_ref, cache_ref, *refs):
    out_ref = refs[-1]
    rows, _, size, half = cache_ref.shape
    positions = 2 * half
    scale = size ** (-0.5)
    chip, core, group = coordinates()
    first = (group * NC + core) * ROWS
    at = lax.broadcasted_iota(jnp.int32, (1, positions), 1)
    own = (chip * NC + core) * half
    other = (chip * NC + 1 - core) * half - half
    start = jnp.where(at < half, own, other)
    base = jnp.minimum(lens[first], 0)
    stats = [[], [], [], []]
    for j in range(rows):
        valid = at < lens[first + j] - start
        weights, pairs = [], []
        for k in range(2):
            lines = [slice(t * 32 + k * GROUP, t * 32 + (k + 1) * GROUP) for t in range(2)]
            q = jnp.concatenate([q_ref[j, part, :] for part in lines], 0)
            keys = jnp.concatenate([cache_ref[j, base + k], cache_ref[j, base + 2 + k]], 1)
            scores = jnp.dot(q, keys, preferred_element_type=F32) * scale
            scores = jnp.where(valid, scores, NEG_FILL)
            high, low = split_pair(jnp.max(scores, 1, keepdims=True))
            weight = jnp.where(valid, jnp.exp(scores - (high + low)), 0.0)
            pairs.append((high, low) + split_pair(jnp.sum(weight, 1, keepdims=True)))
            weights.append(weight.astype(BF16))
        values = jnp.concatenate(
            [
                jnp.concatenate([cache_ref[j, base + 4 + 2 * i], cache_ref[j, base + 5 + 2 * i]], 1)
                for i in range(2)
            ],
            0,
        )
        o = jnp.dot(jnp.concatenate(weights, 0), values, preferred_element_type=F32)
        for t in range(2):
            for k in range(2):
                line = t * 32 + k * GROUP
                part = o[k * 32 + t * GROUP : k * 32 + (t + 1) * GROUP, k * size : (k + 1) * size]
                out_ref[j, line : line + GROUP, :] = part.astype(BF16)
                for i in range(4):
                    stats[i].append(pairs[k][i][t * GROUP : (t + 1) * GROUP])
    stats = [jnp.concatenate(stat, 0) for stat in stats]
    lane = lax.broadcasted_iota(jnp.int32, (rows * LINES, 128), 1)
    table = jnp.where(lane == 0, stats[0], 0.0)
    for i in range(1, 4):
        table = jnp.where(lane == i, stats[i], table)
    table = table.T[:TAIL]
    for j in range(rows):
        tail = table[:, (j // 2) * 128 : (j // 2 + 1) * 128]
        if j % 2 == 1:
            tail = pltpu.roll(tail, LINES, 1)
        out_ref[j, LINES:, :] = tail.astype(BF16)


def attend(lens, queries, cache, before):
    rows, _, size, positions = cache.shape
    return pl.pallas_call(
        attend_kernel,
        in_specs=[SMEM, VMEM, VMEM] + [ANY] * len(before),
        out_specs=VMEM,
        out_shape=jax.ShapeDtypeStruct((rows, BLOCK, size), BF16),
        compiler_params=PARAMS,
        cost_estimate=pl.CostEstimate(
            flops=120 * ROWS * LINES * positions * size,
            bytes_accessed=160 * ROWS * positions * size,
            transcendentals=0,
        ),
    )(lens, queries, cache, *before)


def to_owners_kernel(order, *refs):
    own, other = refs[:NY], refs[NY : 2 * NY]
    out_ref, slots, keep = refs[2 * NY :]
    _, core, y = coordinates()
    for slot in range(CHIPS * NC):
        slots[order[slot]] = slot
    for d in range(NY):
        group = lax.rem(y + d, NY)
        for c, source in ((core, own[d]), (1 - core, other[d])):
            for row in range(ROWS):
                keep[slots[(group * NC + c) * ROWS + row]] = source[row]
    for chip in range(CHIPS):
        out_ref[chip] = keep[chip * NC + core]


def to_owners(order, own, other):
    block = own[0].shape[1:]
    return pl.pallas_call(
        to_owners_kernel,
        in_specs=[SMEM] + [VMEM] * (2 * NY),
        out_specs=VMEM,
        out_shape=jax.ShapeDtypeStruct((CHIPS,) + block, BF16),
        scratch_shapes=[
            pltpu.SMEM((CHIPS * NC,), jnp.int32),
            pltpu.VMEM((CHIPS * NC,) + block, BF16),
        ],
        compiler_params=PARAMS,
    )(order, *own, *other)


def finish_kernel(part_ref, q_ref, key_ref, value_ref, out_ref):
    size = q_ref.shape[1]
    scale = size ** (-0.5)
    tail = part_ref[:, LINES:, :].astype(F32)
    tops = tail[:, 0, :] + tail[:, 1, :]
    totals = tail[:, 2, :] + tail[:, 3, :]
    table = jnp.concatenate([tops, totals, jnp.zeros((128 - 2 * CHIPS, 128), F32)], 0).T[:LINES]
    tops, totals = table[:, :CHIPS], table[:, CHIPS : 2 * CHIPS]
    line = lax.broadcasted_iota(jnp.int32, (LINES, 1), 0)
    step = line // 32
    first = (line % 32) // GROUP == 0
    q = q_ref[...].astype(F32)
    top = jnp.max(tops, 1, keepdims=True)
    scores, values = [], []
    for u in range(2):
        pair = key_ref[u].astype(F32)
        key = jnp.where(first, pair[0:1], pair[1:2])
        pair = value_ref[u].astype(F32)
        values.append(jnp.where(first, pair[0:1], pair[1:2]))
        score = jnp.sum(q * key, -1, keepdims=True) * scale
        scores.append(jnp.where(u <= step, score, NEG_FILL))
        top = jnp.maximum(top, scores[u])
    factors = jnp.exp(tops - top)
    total = jnp.sum(factors * totals, 1, keepdims=True)
    accum = jnp.zeros((LINES, size), F32)
    for chip in range(CHIPS):
        accum = accum + factors[:, chip : chip + 1] * part_ref[chip, :LINES, :].astype(F32)
    for u in range(2):
        weight = jnp.where(u <= step, jnp.exp(scores[u] - top), 0.0)
        total = total + weight
        accum = accum + weight.astype(BF16).astype(F32) * values[u]
    out_ref[...] = (accum / total).astype(BF16)


def finish(parts, queries, new_keys, new_values):
    return pl.pallas_call(
        finish_kernel,
        in_specs=[VMEM] * 4,
        out_specs=VMEM,
        out_shape=jax.ShapeDtypeStruct(queries.shape, BF16),
        compiler_params=PARAMS,
    )(parts, queries, new_keys, new_values)


def over_chips(x):
    groups = [[chip * NC + c for chip in range(CHIPS)] for c in range(NC)]
    return lax.all_to_all(
        x, "seq", split_axis=0, concat_axis=0, axis_index_groups=groups, tiled=True
    )


def along_kvh(x, d):
    return lax.ppermute(x, "kvh", [(y, (y + d) % NY) for y in range(NY)])


def to_other_core(x):
    return lax.ppermute(x, "seq", [(i, i ^ 1) for i in range(CHIPS * NC)])


def on_device(queries, new_keys, new_values, cache_keys, cache_values, decode_order, cache_len):
    size = queries.shape[-1]

    other_keys, other_values = to_other_core(cache_keys), to_other_core(cache_values)

    own = queries.reshape(LINES, size)
    send, core = spread(own)
    got = over_chips(send)
    caches, token = by_head(core, (cache_keys, other_keys), (cache_values, other_values))
    sends = to_groups(decode_order, got, to_other_core(pass_on(token, got)))

    parts = [None] * NY
    near = (1, 3, 2, 0)
    gots = {d: along_kvh(sends[d], d) if d else sends[d] for d in near}
    before = ()
    for d in near:
        part = attend(cache_len, gots[d], caches[d], before)
        before = (part,)
        parts[d] = along_kvh(part, NY - d) if d else part

    part = over_chips(to_owners(decode_order, parts, [to_other_core(part) for part in parts]))
    out = finish(part, own, new_keys[0], new_values[0])
    return out.reshape(queries.shape)


def solution(mesh):
    return jax.shard_map(
        on_device,
        mesh=mesh,
        in_specs=(
            P("seq", None, "kvh", None),
            P("seq", None, "kvh", None),
            P("seq", None, "kvh", None),
            P("kvh", "seq", None, None),
            P("kvh", "seq", None, None),
            P(),
            P(),
        ),
        out_specs=P("seq", None, "kvh", None),
        check_vma=False,
    )
```

```python
import jax
import jax.numpy as jnp
from jax import lax
from jax.experimental import pallas as pl
from jax.experimental.pallas import tpu as pltpu
from jax.sharding import PartitionSpec as P

NEG_FILL = -1e30
NC, NY = 2, 4
CHIPS = 32
GROUP = 16
ROWS = 8
LINES = 64
TAIL = 8
NEAR = (0, 2, 3, 1)
BLOCK = LINES + TAIL
F32 = jnp.float32
BF16 = jnp.bfloat16
SMEM = pl.BlockSpec(memory_space=pltpu.SMEM)
VMEM = pl.BlockSpec(memory_space=pltpu.VMEM)
PARAMS = pltpu.CompilerParams(vmem_limit_bytes=16 * 2**20)
BRINGING = pl.CostEstimate(flops=2**30, bytes_accessed=2**24, transcendentals=0)


def split_pair(x):
    high = x.astype(BF16).astype(F32)
    low = (x - high).astype(BF16).astype(F32)
    return high, low


def coordinates():
    s = lax.axis_index("seq")
    return s // NC, lax.rem(s, NC), lax.axis_index("kvh")


def spread_kernel(own_ref, out_ref, core_ref):
    for chip in range(CHIPS):
        out_ref[chip] = own_ref[...]
    core_ref[0] = coordinates()[1]


def spread(own):
    return pl.pallas_call(
        spread_kernel,
        in_specs=[VMEM],
        out_specs=[VMEM, SMEM],
        out_shape=[
            jax.ShapeDtypeStruct((CHIPS,) + own.shape, BF16),
            jax.ShapeDtypeStruct((1,), jnp.int32),
        ],
        compiler_params=PARAMS,
    )(own)


def pass_on_kernel(token, got_ref, out_ref):
    out_ref[...] = got_ref[...]


def pass_on(token, got):
    return pl.pallas_call(
        pass_on_kernel,
        in_specs=[SMEM, VMEM],
        out_specs=VMEM,
        out_shape=jax.ShapeDtypeStruct(got.shape, got.dtype),
        compiler_params=PARAMS,
        cost_estimate=BRINGING,
    )(token, got)


def to_groups_kernel(order, own_ref, other_ref, *refs):
    outs, slots = refs[:NY], refs[NY]
    _, core, y = coordinates()
    for slot in range(CHIPS * NC):
        slots[order[slot]] = slot
    for out, d in zip(outs, NEAR):
        group = lax.rem(y + d, NY)
        for row in range(ROWS):
            slot = slots[(group * NC + core) * ROWS + row]
            chip = slot // NC
            mine = lax.rem(slot, NC) == core
            out[row] = jnp.where(mine, own_ref[chip], other_ref[chip])


def to_groups(order, own, other):
    _, lines, size = own.shape
    return pl.pallas_call(
        to_groups_kernel,
        in_specs=[SMEM, VMEM, VMEM],
        out_specs=[VMEM] * NY,
        out_shape=[jax.ShapeDtypeStruct((ROWS, lines, size), BF16)] * NY,
        scratch_shapes=[pltpu.SMEM((CHIPS * NC,), jnp.int32)],
        compiler_params=PARAMS,
        cost_estimate=BRINGING,
    )(order, own, other)


def by_head_kernel(core, *refs):
    ins, outs = refs[:4], refs[4 : 4 + NY]
    token, keep = refs[-2:]
    _, positions, kv, size = ins[0].shape
    y = coordinates()[2]
    token[0] = core[0]
    for slot in range(4):
        keep[slot] = ins[slot][0].reshape(positions * kv, size).astype(F32)
    for out, d in zip(outs, NEAR):
        quarter = lax.rem(y + NY - d, NY)
        for k in range(2):
            head = pl.ds(2 * quarter + k, positions, stride=kv)
            for i in range(2):
                out[0, i * 2 + k] = keep[i, head, :].astype(BF16).T
                out[0, 4 + i * 2 + k] = keep[2 + i, head, :].astype(BF16)


def by_head(core, keys, values):
    _, positions, kv, size = keys[0].shape
    rows = pl.BlockSpec((1, positions, kv, size), lambda i, core: (core[0] * ROWS + i, 0, 0, 0))
    tiles = (8, size, positions)
    outs = pl.pallas_call(
        by_head_kernel,
        grid_spec=pltpu.PrefetchScalarGridSpec(
            num_scalar_prefetch=1,
            grid=(ROWS,),
            in_specs=[rows] * 4,
            out_specs=[pl.BlockSpec((1,) + tiles, lambda i, core: (i, 0, 0, 0))] * NY + [SMEM],
            scratch_shapes=[pltpu.VMEM((4, positions * kv, size), F32)],
        ),
        out_shape=[jax.ShapeDtypeStruct((ROWS,) + tiles, BF16)] * NY
        + [jax.ShapeDtypeStruct((1,), jnp.int32)],
        cost_estimate=pl.CostEstimate(
            flops=0, bytes_accessed=16 * ROWS * positions * kv * size, transcendentals=0
        ),
    )(core, *keys, *values)
    return outs[:NY], outs[NY]


def attend_kernel(lens, q_ref, cache_ref, out_ref):
    rows, _, size, half = cache_ref.shape
    positions = 2 * half
    scale = size ** (-0.5)
    chip, core, group = coordinates()
    first = (group * NC + core) * ROWS
    at = lax.broadcasted_iota(jnp.int32, (1, positions), 1)
    own = (chip * NC + core) * half
    other = (chip * NC + 1 - core) * half - half
    start = jnp.where(at < half, own, other)
    base = jnp.minimum(lens[first], 0)
    stats = [[], [], [], []]
    for j in range(rows):
        valid = at < lens[first + j] - start
        weights, pairs = [], []
        for k in range(2):
            lines = [slice(t * 32 + k * GROUP, t * 32 + (k + 1) * GROUP) for t in range(2)]
            q = jnp.concatenate([q_ref[j, part, :] for part in lines], 0)
            keys = jnp.concatenate([cache_ref[j, base + k], cache_ref[j, base + 2 + k]], 1)
            scores = jnp.dot(q, keys, preferred_element_type=F32) * scale
            scores = jnp.where(valid, scores, NEG_FILL)
            high, low = split_pair(jnp.max(scores, 1, keepdims=True))
            weight = jnp.where(valid, jnp.exp(scores - (high + low)), 0.0)
            pairs.append((high, low) + split_pair(jnp.sum(weight, 1, keepdims=True)))
            weights.append(weight.astype(BF16))
        values = jnp.concatenate(
            [
                jnp.concatenate([cache_ref[j, base + 4 + 2 * i], cache_ref[j, base + 5 + 2 * i]], 1)
                for i in range(2)
            ],
            0,
        )
        o = jnp.dot(jnp.concatenate(weights, 0), values, preferred_element_type=F32)
        for t in range(2):
            for k in range(2):
                line = t * 32 + k * GROUP
                part = o[k * 32 + t * GROUP : k * 32 + (t + 1) * GROUP, k * size : (k + 1) * size]
                out_ref[j, line : line + GROUP, :] = part.astype(BF16)
                for i in range(4):
                    stats[i].append(pairs[k][i][t * GROUP : (t + 1) * GROUP])
    stats = [jnp.concatenate(stat, 0) for stat in stats]
    lane = lax.broadcasted_iota(jnp.int32, (rows * LINES, 128), 1)
    table = jnp.where(lane == 0, stats[0], 0.0)
    for i in range(1, 4):
        table = jnp.where(lane == i, stats[i], table)
    table = table.T[:TAIL]
    for j in range(rows):
        tail = table[:, (j // 2) * 128 : (j // 2 + 1) * 128]
        if j % 2 == 1:
            tail = pltpu.roll(tail, LINES, 1)
        out_ref[j, LINES:, :] = tail.astype(BF16)


def attend(lens, queries, cache):
    rows, _, size, positions = cache.shape
    return pl.pallas_call(
        attend_kernel,
        in_specs=[SMEM, VMEM, VMEM],
        out_specs=VMEM,
        out_shape=jax.ShapeDtypeStruct((rows, BLOCK, size), BF16),
        compiler_params=PARAMS,
        cost_estimate=pl.CostEstimate(
            flops=120 * ROWS * LINES * positions * size,
            bytes_accessed=160 * ROWS * positions * size,
            transcendentals=0,
        ),
    )(lens, queries, cache)


def to_owners_kernel(order, *refs):
    own, other = refs[:NY], refs[NY : 2 * NY]
    out_ref, slots, keep = refs[2 * NY :]
    _, core, y = coordinates()
    for slot in range(CHIPS * NC):
        slots[order[slot]] = slot
    for i, d in enumerate(NEAR):
        group = lax.rem(y + d, NY)
        for c, source in ((core, own[i]), (1 - core, other[i])):
            for row in range(ROWS):
                keep[slots[(group * NC + c) * ROWS + row]] = source[row]
    for chip in range(CHIPS):
        out_ref[chip] = keep[chip * NC + core]


def to_owners(order, own, other):
    block = own[0].shape[1:]
    return pl.pallas_call(
        to_owners_kernel,
        in_specs=[SMEM] + [VMEM] * (2 * NY),
        out_specs=VMEM,
        out_shape=jax.ShapeDtypeStruct((CHIPS,) + block, BF16),
        scratch_shapes=[
            pltpu.SMEM((CHIPS * NC,), jnp.int32),
            pltpu.VMEM((CHIPS * NC,) + block, BF16),
        ],
        compiler_params=PARAMS,
    )(order, *own, *other)


def finish_kernel(part_ref, q_ref, key_ref, value_ref, out_ref):
    size = q_ref.shape[1]
    scale = size ** (-0.5)
    tail = part_ref[:, LINES:, :].astype(F32)
    tops = tail[:, 0, :] + tail[:, 1, :]
    totals = tail[:, 2, :] + tail[:, 3, :]
    table = jnp.concatenate([tops, totals, jnp.zeros((128 - 2 * CHIPS, 128), F32)], 0).T[:LINES]
    tops, totals = table[:, :CHIPS], table[:, CHIPS : 2 * CHIPS]
    line = lax.broadcasted_iota(jnp.int32, (LINES, 1), 0)
    step = line // 32
    first = (line % 32) // GROUP == 0
    q = q_ref[...].astype(F32)
    top = jnp.max(tops, 1, keepdims=True)
    scores, values = [], []
    for u in range(2):
        pair = key_ref[u].astype(F32)
        key = jnp.where(first, pair[0:1], pair[1:2])
        pair = value_ref[u].astype(F32)
        values.append(jnp.where(first, pair[0:1], pair[1:2]))
        score = jnp.sum(q * key, -1, keepdims=True) * scale
        scores.append(jnp.where(u <= step, score, NEG_FILL))
        top = jnp.maximum(top, scores[u])
    factors = jnp.exp(tops - top)
    total = jnp.sum(factors * totals, 1, keepdims=True)
    accum = jnp.zeros((LINES, size), F32)
    for chip in range(CHIPS):
        accum = accum + factors[:, chip : chip + 1] * part_ref[chip, :LINES, :].astype(F32)
    for u in range(2):
        weight = jnp.where(u <= step, jnp.exp(scores[u] - top), 0.0)
        total = total + weight
        accum = accum + weight.astype(BF16).astype(F32) * values[u]
    out_ref[...] = (accum / total).astype(BF16)


def finish(parts, queries, new_keys, new_values):
    return pl.pallas_call(
        finish_kernel,
        in_specs=[VMEM] * 4,
        out_specs=VMEM,
        out_shape=jax.ShapeDtypeStruct(queries.shape, BF16),
        compiler_params=PARAMS,
    )(parts, queries, new_keys, new_values)


def over_chips(x):
    groups = [[chip * NC + c for chip in range(CHIPS)] for c in range(NC)]
    return lax.all_to_all(
        x, "seq", split_axis=0, concat_axis=0, axis_index_groups=groups, tiled=True
    )


def along_kvh(x, d):
    return lax.ppermute(x, "kvh", [(y, (y + d) % NY) for y in range(NY)])


def to_other_core(x):
    return lax.ppermute(x, "seq", [(i, i ^ 1) for i in range(CHIPS * NC)])


def on_device(queries, new_keys, new_values, cache_keys, cache_values, decode_order, cache_len):
    size = queries.shape[-1]

    other_keys, other_values = to_other_core(cache_keys), to_other_core(cache_values)

    own = queries.reshape(LINES, size)
    send, core = spread(own)
    got = over_chips(send)
    caches, token = by_head(core, (cache_keys, other_keys), (cache_values, other_values))
    sends = to_groups(decode_order, got, to_other_core(pass_on(token, got)))

    parts = []
    for d, send, cache in zip(NEAR, sends, caches):
        part = attend(cache_len, along_kvh(send, d) if d else send, cache)
        parts.append(along_kvh(part, NY - d) if d else part)

    part = over_chips(to_owners(decode_order, parts, [to_other_core(part) for part in parts]))
    out = finish(part, own, new_keys[0], new_values[0])
    return out.reshape(queries.shape)


def solution(mesh):
    return jax.shard_map(
        on_device,
        mesh=mesh,
        in_specs=(
            P("seq", None, "kvh", None),
            P("seq", None, "kvh", None),
            P("seq", None, "kvh", None),
            P("kvh", "seq", None, None),
            P("kvh", "seq", None, None),
            P(),
            P(),
        ),
        out_specs=P("seq", None, "kvh", None),
        check_vma=False,
    )
```

```python
import jax
import jax.numpy as jnp
from jax import lax
from jax.experimental import pallas as pl
from jax.experimental.pallas import tpu as pltpu
from jax.sharding import PartitionSpec as P

NEG_FILL = -1e30
NC, NY = 2, 4
CHIPS = 32
GROUP = 16
ROWS = 8
LINES = 64
TAIL = 8
BLOCK = LINES + TAIL
F32 = jnp.float32
BF16 = jnp.bfloat16
SMEM = pl.BlockSpec(memory_space=pltpu.SMEM)
VMEM = pl.BlockSpec(memory_space=pltpu.VMEM)
ANY = pl.BlockSpec(memory_space=pl.ANY)
PARAMS = pltpu.CompilerParams(vmem_limit_bytes=16 * 2**20)
BRINGING = pl.CostEstimate(flops=2**30, bytes_accessed=2**24, transcendentals=0)


def split_pair(x):
    high = x.astype(BF16).astype(F32)
    low = (x - high).astype(BF16).astype(F32)
    return high, low


def coordinates():
    s = lax.axis_index("seq")
    return s // NC, lax.rem(s, NC), lax.axis_index("kvh")


def spread_kernel(own_ref, out_ref, core_ref):
    for chip in range(CHIPS):
        out_ref[chip] = own_ref[...]
    core_ref[0] = coordinates()[1]


def spread(own):
    return pl.pallas_call(
        spread_kernel,
        in_specs=[VMEM],
        out_specs=[VMEM, SMEM],
        out_shape=[
            jax.ShapeDtypeStruct((CHIPS,) + own.shape, BF16),
            jax.ShapeDtypeStruct((1,), jnp.int32),
        ],
        compiler_params=PARAMS,
    )(own)


def pass_on_kernel(token, got_ref, out_ref):
    out_ref[...] = got_ref[...]


def pass_on(token, got):
    return pl.pallas_call(
        pass_on_kernel,
        in_specs=[SMEM, VMEM],
        out_specs=VMEM,
        out_shape=jax.ShapeDtypeStruct(got.shape, got.dtype),
        compiler_params=PARAMS,
        cost_estimate=BRINGING,
    )(token, got)


def to_groups_kernel(order, own_ref, other_ref, *refs):
    outs, slots = refs[:NY], refs[NY]
    _, core, y = coordinates()
    for slot in range(CHIPS * NC):
        slots[order[slot]] = slot
    for d in range(NY):
        group = lax.rem(y + d, NY)
        for row in range(ROWS):
            slot = slots[(group * NC + core) * ROWS + row]
            chip = slot // NC
            mine = lax.rem(slot, NC) == core
            outs[d][row] = jnp.where(mine, own_ref[chip], other_ref[chip])


def to_groups(order, own, other):
    _, lines, size = own.shape
    return pl.pallas_call(
        to_groups_kernel,
        in_specs=[SMEM, VMEM, VMEM],
        out_specs=[VMEM] * NY,
        out_shape=[jax.ShapeDtypeStruct((ROWS, lines, size), BF16)] * NY,
        scratch_shapes=[pltpu.SMEM((CHIPS * NC,), jnp.int32)],
        compiler_params=PARAMS,
        cost_estimate=BRINGING,
    )(order, own, other)


def by_head_kernel(core, *refs):
    ins, outs = refs[:4], refs[4 : 4 + NY]
    token, keep = refs[-2:]
    _, positions, kv, size = ins[0].shape
    y = coordinates()[2]
    token[0] = core[0]
    for slot in range(4):
        keep[slot] = ins[slot][0].reshape(positions * kv, size).astype(F32)
    for d in range(NY):
        quarter = lax.rem(y + NY - d, NY)
        for k in range(2):
            head = pl.ds(2 * quarter + k, positions, stride=kv)
            for i in range(2):
                outs[d][0, i * 2 + k] = keep[i, head, :].astype(BF16).T
                outs[d][0, 4 + i * 2 + k] = keep[2 + i, head, :].astype(BF16)


def by_head(core, keys, values):
    _, positions, kv, size = keys[0].shape
    rows = pl.BlockSpec((1, positions, kv, size), lambda i, core: (core[0] * ROWS + i, 0, 0, 0))
    tiles = (8, size, positions)
    outs = pl.pallas_call(
        by_head_kernel,
        grid_spec=pltpu.PrefetchScalarGridSpec(
            num_scalar_prefetch=1,
            grid=(ROWS,),
            in_specs=[rows] * 4,
            out_specs=[pl.BlockSpec((1,) + tiles, lambda i, core: (i, 0, 0, 0))] * NY + [SMEM],
            scratch_shapes=[pltpu.VMEM((4, positions * kv, size), F32)],
        ),
        out_shape=[jax.ShapeDtypeStruct((ROWS,) + tiles, BF16)] * NY
        + [jax.ShapeDtypeStruct((1,), jnp.int32)],
        cost_estimate=pl.CostEstimate(
            flops=0, bytes_accessed=16 * ROWS * positions * kv * size, transcendentals=0
        ),
    )(core, *keys, *values)
    return outs[:NY], outs[NY]


def attend_kernel(picked, lens, q_ref, cache_ref, *refs):
    out_ref = refs[-1]
    _, _, size, half = cache_ref.shape
    positions = 2 * half
    scale = size ** (-0.5)
    chip, core, group = coordinates()
    first = (group * NC + core) * ROWS
    at = lax.broadcasted_iota(jnp.int32, (1, positions), 1)
    own = (chip * NC + core) * half
    other = (chip * NC + 1 - core) * half - half
    start = jnp.where(at < half, own, other)
    base = jnp.minimum(lens[first], 0)
    stats = [[], [], [], []]
    for j in picked:
        valid = at < lens[first + j] - start
        weights, pairs = [], []
        for k in range(2):
            lines = [slice(t * 32 + k * GROUP, t * 32 + (k + 1) * GROUP) for t in range(2)]
            q = jnp.concatenate([q_ref[j, part, :] for part in lines], 0)
            keys = jnp.concatenate([cache_ref[j, base + k], cache_ref[j, base + 2 + k]], 1)
            scores = jnp.dot(q, keys, preferred_element_type=F32) * scale
            scores = jnp.where(valid, scores, NEG_FILL)
            high, low = split_pair(jnp.max(scores, 1, keepdims=True))
            weight = jnp.where(valid, jnp.exp(scores - (high + low)), 0.0)
            pairs.append((high, low) + split_pair(jnp.sum(weight, 1, keepdims=True)))
            weights.append(weight.astype(BF16))
        values = jnp.concatenate(
            [
                jnp.concatenate([cache_ref[j, base + 4 + 2 * i], cache_ref[j, base + 5 + 2 * i]], 1)
                for i in range(2)
            ],
            0,
        )
        o = jnp.dot(jnp.concatenate(weights, 0), values, preferred_element_type=F32)
        for t in range(2):
            for k in range(2):
                line = t * 32 + k * GROUP
                part = o[k * 32 + t * GROUP : k * 32 + (t + 1) * GROUP, k * size : (k + 1) * size]
                out_ref[j, line : line + GROUP, :] = part.astype(BF16)
                for i in range(4):
                    stats[i].append(pairs[k][i][t * GROUP : (t + 1) * GROUP])
    stats = [jnp.concatenate(stat, 0) for stat in stats]
    lane = lax.broadcasted_iota(jnp.int32, (len(picked) * LINES, 128), 1)
    table = jnp.where(lane == 0, stats[0], 0.0)
    for i in range(1, 4):
        table = jnp.where(lane == i, stats[i], table)
    table = table.T[:TAIL]
    for n, j in enumerate(picked):
        tail = table[:, (n // 2) * 128 : (n // 2 + 1) * 128]
        if n % 2 == 1:
            tail = pltpu.roll(tail, LINES, 1)
        out_ref[j, LINES:, :] = tail.astype(BF16)


def attend(lens, queries, cache, before, picked=range(ROWS), done=()):
    _, _, size, positions = cache.shape

    def kernel(lens, q_ref, cache_ref, *refs):
        if done:
            refs[-1][: picked[0]] = refs[0][...]
        attend_kernel(picked, lens, q_ref, cache_ref, *refs)

    return pl.pallas_call(
        kernel,
        in_specs=[SMEM, VMEM, VMEM] + [VMEM] * len(done) + [ANY] * len(before),
        out_specs=VMEM,
        out_shape=jax.ShapeDtypeStruct((picked[-1] + 1, BLOCK, size), BF16),
        compiler_params=PARAMS,
        cost_estimate=pl.CostEstimate(
            flops=120 * ROWS * LINES * positions * size,
            bytes_accessed=160 * ROWS * positions * size,
            transcendentals=0,
        ),
    )(lens, queries, cache, *done, *before)


def to_owners_kernel(order, *refs):
    own, other = refs[:NY], refs[NY : 2 * NY]
    out_ref, slots, keep = refs[2 * NY :]
    _, core, y = coordinates()
    for slot in range(CHIPS * NC):
        slots[order[slot]] = slot
    for d in range(NY):
        group = lax.rem(y + d, NY)
        for c, source in ((core, own[d]), (1 - core, other[d])):
            for row in range(ROWS):
                keep[slots[(group * NC + c) * ROWS + row]] = source[row]
    for chip in range(CHIPS):
        out_ref[chip] = keep[chip * NC + core]


def to_owners(order, own, other):
    block = own[0].shape[1:]
    return pl.pallas_call(
        to_owners_kernel,
        in_specs=[SMEM] + [VMEM] * (2 * NY),
        out_specs=VMEM,
        out_shape=jax.ShapeDtypeStruct((CHIPS,) + block, BF16),
        scratch_shapes=[
            pltpu.SMEM((CHIPS * NC,), jnp.int32),
            pltpu.VMEM((CHIPS * NC,) + block, BF16),
        ],
        compiler_params=PARAMS,
    )(order, *own, *other)


def finish_kernel(part_ref, q_ref, key_ref, value_ref, out_ref):
    size = q_ref.shape[1]
    scale = size ** (-0.5)
    tail = part_ref[:, LINES:, :].astype(F32)
    tops = tail[:, 0, :] + tail[:, 1, :]
    totals = tail[:, 2, :] + tail[:, 3, :]
    table = jnp.concatenate([tops, totals, jnp.zeros((128 - 2 * CHIPS, 128), F32)], 0).T[:LINES]
    tops, totals = table[:, :CHIPS], table[:, CHIPS : 2 * CHIPS]
    line = lax.broadcasted_iota(jnp.int32, (LINES, 1), 0)
    step = line // 32
    first = (line % 32) // GROUP == 0
    q = q_ref[...].astype(F32)
    top = jnp.max(tops, 1, keepdims=True)
    scores, values = [], []
    for u in range(2):
        pair = key_ref[u].astype(F32)
        key = jnp.where(first, pair[0:1], pair[1:2])
        pair = value_ref[u].astype(F32)
        values.append(jnp.where(first, pair[0:1], pair[1:2]))
        score = jnp.sum(q * key, -1, keepdims=True) * scale
        scores.append(jnp.where(u <= step, score, NEG_FILL))
        top = jnp.maximum(top, scores[u])
    factors = jnp.exp(tops - top)
    total = jnp.sum(factors * totals, 1, keepdims=True)
    accum = jnp.zeros((LINES, size), F32)
    for chip in range(CHIPS):
        accum = accum + factors[:, chip : chip + 1] * part_ref[chip, :LINES, :].astype(F32)
    for u in range(2):
        weight = jnp.where(u <= step, jnp.exp(scores[u] - top), 0.0)
        total = total + weight
        accum = accum + weight.astype(BF16).astype(F32) * values[u]
    out_ref[...] = (accum / total).astype(BF16)


def finish(parts, queries, new_keys, new_values):
    return pl.pallas_call(
        finish_kernel,
        in_specs=[VMEM] * 4,
        out_specs=VMEM,
        out_shape=jax.ShapeDtypeStruct(queries.shape, BF16),
        compiler_params=PARAMS,
    )(parts, queries, new_keys, new_values)


def over_chips(x):
    groups = [[chip * NC + c for chip in range(CHIPS)] for c in range(NC)]
    return lax.all_to_all(
        x, "seq", split_axis=0, concat_axis=0, axis_index_groups=groups, tiled=True
    )


def along_kvh(x, d):
    return lax.ppermute(x, "kvh", [(y, (y + d) % NY) for y in range(NY)])


def to_other_core(x):
    return lax.ppermute(x, "seq", [(i, i ^ 1) for i in range(CHIPS * NC)])


def on_device(queries, new_keys, new_values, cache_keys, cache_values, decode_order, cache_len):
    size = queries.shape[-1]

    other_keys, other_values = to_other_core(cache_keys), to_other_core(cache_values)

    own = queries.reshape(LINES, size)
    send, core = spread(own)
    got = over_chips(send)
    caches, token = by_head(core, (cache_keys, other_keys), (cache_values, other_values))
    sends = to_groups(decode_order, got, to_other_core(pass_on(token, got)))

    parts = [None] * NY
    near = (1, 3, 2)
    gots = {d: along_kvh(sends[d], d) for d in near}
    half = attend(cache_len, sends[0], caches[0], (), range(ROWS // 2))
    before = (half,)
    for d in near:
        part = attend(cache_len, gots[d], caches[d], before)
        before = (part,)
        parts[d] = along_kvh(part, NY - d)
    rest = range(ROWS // 2, ROWS)
    parts[0] = attend(cache_len, sends[0], caches[0], before, rest, (half,))

    part = over_chips(to_owners(decode_order, parts, [to_other_core(part) for part in parts]))
    out = finish(part, own, new_keys[0], new_values[0])
    return out.reshape(queries.shape)


def solution(mesh):
    return jax.shard_map(
        on_device,
        mesh=mesh,
        in_specs=(
            P("seq", None, "kvh", None),
            P("seq", None, "kvh", None),
            P("seq", None, "kvh", None),
            P("kvh", "seq", None, None),
            P("kvh", "seq", None, None),
            P(),
            P(),
        ),
        out_specs=P("seq", None, "kvh", None),
        check_vma=False,
    )
```
